256 devices in a mesh: row: 32 (over z_hi, x, core), feat: 8 (over z_lo, y).
Axes of the slice: x: 4, y: 4, z: 8 (z_hi: 4, z_lo: 2; z = z_hi * 2 + z_lo), core: 2. Of those that a mesh axis runs over, the one named last changes fastest.
Arguments:
- features: bfloat16 [131072, 8192], P('row', 'feat'), may hold values from -6 to 6
- coef: bfloat16 [8192], P('feat'), may hold values from -0.0625 to 0.0625
- labels: int32 [131072], P('row'), may hold values 0 or 1
- sign_bits: int32 [131072], P('row'), may hold values 0 or 1
- samples: int32 [32, 4096], P('row'), may hold values from 0 to 4095
Outputs:
- gradient: float32 [8192], P('feat')
- sketch: bfloat16 [4096, 8192], P('row', 'feat')
- gram: float32 [4096, 4096], P('row', 'feat')
The draws below stay inside these ranges and needn't reach their ends.
Inputs may be any that keep to these rules, and one draw needn't show every extreme that they name: `samples`: row index inside the block.
All inputs are finite; a program needn't handle non-finite values. No bound on the sum of `labels` or of `sign_bits` on one device may be relied on, other than what follows from the above.
Results may differ from the reference program's by a relative error of at most 0.017.
Values may be sent and summed in bfloat16 or wider, within the bound.
No kernel may reach another device: no remote copies, remote signals or barrier semaphores. Data moves between devices by JAX's collectives and lax.ppermute only.
A program may use at most 128 MiB of HBM per device.

```python
import jax
import jax.numpy as jnp
from jax import lax

F = 8192
SKETCH = 4096
ROWS_DEV = 4096
BLOCKS = 32
TOTAL = 131072


def with_ends(values, stream_key, smallest, largest):
    dims = values.shape
    spot = [jax.random.randint(jax.random.fold_in(stream_key, axis), (), 0, dims[axis]) for axis in range(len(dims))]
    values = values.at[tuple(spot)].set(smallest)
    longest = dims.index(max(dims))
    spot[longest] = (spot[longest] + 1) % dims[longest]
    return values.at[tuple(spot)].set(largest)


def block_levels(key, extent, split, low, top_value):
    loudness = 1.0
    for position, shards_of in split:
        heights = jax.random.uniform(jax.random.fold_in(jax.random.fold_in(key, 6), position), (shards_of,), jnp.float32, low / len(split), top_value / len(split))
        loudness = loudness * jnp.repeat(jnp.exp(heights), extent[position] // shards_of).reshape((-1,) + (1,) * (len(extent) - 1 - position))
    return loudness


def gaussian(own_key, extent, spread, bound, shards=(), kind=jnp.bfloat16):
    drawn = jax.random.normal(own_key, extent, jnp.float32) * spread
    if len(shards) > 0:
        drawn = block_levels(own_key, extent, shards, -0.22, 0.18) * drawn
    return jnp.clip(drawn, min=-bound, max=bound).astype(kind)


def setup_inputs(seed: int = 0) -> dict:
    streams_of = jax.random.split(jax.random.key(seed), 6)
    return {
        "features": gaussian(streams_of[0], (TOTAL, F), 1.0, 6.0, ((0, 32), (1, 8))),
        "coef": gaussian(streams_of[1], (F,), F ** -0.5, 0.0625, ((0, 8),)),
        "labels": with_ends((jax.random.randint(streams_of[2], (TOTAL,), 0, 2) < 1).astype(jnp.int32), jax.random.fold_in(streams_of[2], 1), 0, 1),
        "sign_bits": with_ends((jax.random.randint(streams_of[3], (TOTAL,), 0, 2) < 1).astype(jnp.int32), jax.random.fold_in(streams_of[3], 1), 0, 1),
        "samples": with_ends(jax.random.randint(streams_of[4], (BLOCKS, SKETCH), 0, ROWS_DEV), jax.random.fold_in(streams_of[4], 1), 0, ROWS_DEV - 1).astype(jnp.int32),
    }


def sylvester(hadamard_order):
    positions = jnp.arange(hadamard_order, dtype=jnp.int32)
    bit_correlation = positions[:, None] & positions[None, :]
    parity_count = jnp.zeros_like(bit_correlation)
    for bit_pos in range(max(hadamard_order.bit_length() - 1, 0)):
        parity_count = parity_count + (bit_correlation >> bit_pos & 1)
    return (1 - 2 * (parity_count % 2)).astype(jnp.float32)

def transform_block(block_rows):
    big_order = 32
    small_order = block_rows.shape[0] // big_order
    high_table = sylvester(big_order)
    low_table = sylvester(small_order)
    shaped = block_rows.reshape(big_order, small_order, block_rows.shape[1])
    first_pass = jnp.einsum('ij,jkf->ikf', high_table, shaped, precision=lax.Precision.HIGHEST)
    second_pass = jnp.einsum('kl,ilf->ikf', low_table, first_pass, precision=lax.Precision.HIGHEST)
    return second_pass.reshape(block_rows.shape[0], block_rows.shape[1])

def reference(features, coef, labels, sign_bits, samples):
    margins = jnp.dot(features, coef, preferred_element_type=jnp.float32)
    probability = jax.nn.sigmoid(margins)
    row_scale = jnp.sqrt(probability * (1.0 - probability))
    residual = (probability - labels.astype(jnp.float32)).astype(jnp.bfloat16)
    root_total = jnp.sqrt(jnp.float32(TOTAL))
    gradient = jnp.dot(residual, features, preferred_element_type=jnp.float32) / root_total
    factors = (2.0 * sign_bits.astype(jnp.float32) - 1.0) * row_scale
    blocks = features.reshape(BLOCKS, ROWS_DEV, F)
    factor_blocks = factors.reshape(BLOCKS, ROWS_DEV)

    def add_block(carry, inputs):
        block_rows, block_factor, block_samples = inputs
        weighted = (block_factor[:, None] * block_rows.astype(jnp.float32)).astype(jnp.bfloat16)
        transformed = transform_block(weighted.astype(jnp.float32))
        picked = lax.optimization_barrier(jnp.take(transformed, block_samples, axis=0).astype(jnp.bfloat16))
        return (carry + picked.astype(jnp.float32), None)
    total_sum, unused = lax.scan(add_block, jnp.zeros((SKETCH, F), jnp.float32), (blocks, factor_blocks, samples))
    sketch = (total_sum / root_total).astype(jnp.bfloat16)
    gram = jnp.dot(sketch, sketch.T, preferred_element_type=jnp.float32) / F
    return (gradient, sketch, gram)
```

```python
import functools

import jax
import jax.numpy as jnp
from jax import lax
from jax.experimental import pallas as pl
from jax.experimental.pallas import tpu as pltpu
from jax.sharding import Mesh, PartitionSpec as P

ROWS = 4096
COLS = 1024
LOW = 256
HIGH = ROWS // LOW
GROUP = 256
LANE_TILES = COLS // 128
HALF_PAIRS = 32
UNROLL = 16
EXTRA = 16


def ring(axis_name, value, shift):
    size = lax.axis_size(axis_name)
    return lax.ppermute(value, axis_name, [(i, (i + shift) % size) for i in range(size)])


def sketch_kernel(spots, own_ref, other_ref, factor_ref, residual_ref, *refs):
    outs, (gradient, table_rows, own_pass, other_pass, transformed) = refs[:8], refs[8:]
    step = pl.program_id(0)
    last = COLS // GROUP

    def multiply(block, high):
        source, target = ((own_ref, own_pass), (other_ref, other_pass))[block]
        product = jnp.dot(
            table_rows[block * HIGH + high],
            source[pl.ds(pl.multiple_of(high * LOW, LOW), LOW), :],
            preferred_element_type=jnp.float32,
        )
        target[high] = product[:LOW]
        gradient[step] += product[LOW : LOW + 8]

    def combine(block, group, tile_row):
        source = (own_pass, other_pass)[block]
        for lane_tile in range(GROUP // 128):
            rows = pl.ds(pl.multiple_of(tile_row * 8, 8), 8)
            values = [source[high, rows, lane_tile * 128 : (lane_tile + 1) * 128] for high in range(HIGH)]
            stride = 1
            while stride < HIGH:
                for high in range(HIGH):
                    if not high & stride:
                        a, b = values[high], values[high + stride]
                        values[high], values[high + stride] = a + b, a - b
                stride *= 2
            place = tile_row * 64 + (group * (GROUP // 128) + lane_tile) * 8
            for high in range(HIGH):
                transformed[block, pl.ds(pl.multiple_of(high * (LOW * 8) + place, 8), 8), :] = values[high]

    def run(multiplied, combined):
        def body(high, carry):
            if multiplied is not None:
                multiply(multiplied, high)
            if combined is not None:
                for tile in range(LOW // 8 // HIGH):
                    combine(*combined, high * (LOW // 8 // HIGH) + tile)
            return carry

        lax.fori_loop(0, HIGH, body, 0, unroll=UNROLL)

    @pl.when(step == 0)
    def _():
        both = lax.broadcasted_iota(jnp.int32, (LOW, LOW), 0) & lax.broadcasted_iota(jnp.int32, (LOW, LOW), 1)
        for bit in (4, 2, 1):
            both = both ^ (both >> bit)
        signs = (1 - 2 * (both & 1)).astype(jnp.float32)
        for part in range(2 * HIGH):
            table_rows[part, :LOW] = (signs * factor_ref[part : part + 1, :]).astype(jnp.bfloat16)
            table_rows[part, LOW:] = jnp.broadcast_to(residual_ref[part : part + 1, :], (EXTRA, LOW)).astype(
                jnp.bfloat16
            )
        gradient[...] = jnp.zeros_like(gradient)
        run(0, None)

    @pl.when((step > 0) & (step < last))
    def _():
        run(0, (1, step - 1))

    @pl.when(step < last)
    def _():
        run(1, (0, step))

    @pl.when(step == last)
    def _():
        run(None, (1, last - 1))
        start = 0
        for out in outs:
            pairs = out.shape[0]

            def pick(pair, carry, out=out, start=start):
                rows = []
                for member in range(2):
                    at = start + pair * 2 + member
                    rows.append(
                        transformed[0, pl.ds(spots[at], 8, 8), :]
                        + transformed[1, pl.ds(spots[2 * 1024 + at], 8, 8), :]
                    )
                out[pair] = jnp.concatenate(rows, axis=0).astype(jnp.bfloat16)
                return carry

            lax.fori_loop(0, pairs, pick, 0, unroll=16)
            start += 2 * pairs


def sketch_pieces(spots, own, other, factors, residuals):
    pairs = [4 * HALF_PAIRS] * 8
    last = COLS // GROUP - 1
    return pl.pallas_call(
        sketch_kernel,
        grid_spec=pltpu.PrefetchScalarGridSpec(
            num_scalar_prefetch=1,
            grid=(last + 2,),
            in_specs=[
                pl.BlockSpec((ROWS, GROUP), lambda i, s: (0, jnp.minimum(i, last))),
                pl.BlockSpec((ROWS, GROUP), lambda i, s: (0, jnp.minimum(i, last))),
                pl.BlockSpec((2 * HIGH, LOW), lambda i, s: (0, 0)),
                pl.BlockSpec((2 * HIGH, LOW), lambda i, s: (0, 0)),
            ],
            out_specs=[pl.BlockSpec((n, 16, 128), lambda i, s: (0, 0, 0)) for n in pairs]
            + [pl.BlockSpec((COLS // GROUP, 8, GROUP), lambda i, s: (0, 0, 0))],
            scratch_shapes=[
                pltpu.VMEM((2 * HIGH, LOW + EXTRA, LOW), jnp.bfloat16),
                pltpu.VMEM((HIGH, LOW, GROUP), jnp.float32),
                pltpu.VMEM((HIGH, LOW, GROUP), jnp.float32),
                pltpu.VMEM((2, ROWS * LANE_TILES + 64, 128), jnp.float32),
            ],
        ),
        out_shape=[jax.ShapeDtypeStruct((n, 16, 128), jnp.bfloat16) for n in pairs]
        + [jax.ShapeDtypeStruct((COLS // GROUP, 8, GROUP), jnp.float32)],
        compiler_params=pltpu.CompilerParams(vmem_limit_bytes=62 * 1024 * 1024),
        cost_estimate=pl.CostEstimate(flops=4_400_000_000, bytes_accessed=22_000_000, transcendentals=0),
        name="hadamard_pick",
    )(spots, own, other, factors, residuals)


def gram_kernel(place, left_ref, own_ref, other_ref, out, tile):
    my_zh, my_x, my_c = [place[i] for i in range(3)]
    for which, source in enumerate((own_ref, other_ref)):
        core = my_c if which == 0 else 1 - my_c
        for shift in range(4):
            product = lax.dot_general(
                left_ref[...],
                source[shift * 128 : (shift + 1) * 128, :],
                (((1,), (1,)), ((), ())),
                preferred_element_type=jnp.float32,
            )
            for row in range(4):
                tile[lax.rem(my_zh + shift, 4) * 2 + core, lax.rem(my_x + row, 4)] = product[
                    row * 128 : (row + 1) * 128
                ].astype(jnp.bfloat16)
    for target in range(8):
        zh, x_low = target // 2, target % 2
        for i in range(2):
            x_high = lax.rem(my_x + i, 2)
            for core in range(2):
                out[target, i, :, core * 128 : (core + 1) * 128] = tile[zh * 2 + core, x_high * 2 + x_low]


def gram_pieces(place, left, right):
    vmem = pl.BlockSpec(memory_space=pltpu.VMEM)
    return pl.pallas_call(
        gram_kernel,
        in_specs=[pl.BlockSpec(memory_space=pltpu.SMEM)] + [vmem] * 3,
        out_specs=vmem,
        out_shape=jax.ShapeDtypeStruct((8, 2, 128, 256), jnp.bfloat16),
        scratch_shapes=[pltpu.VMEM((8, 4, 128, 128), jnp.bfloat16)],
        compiler_params=pltpu.CompilerParams(vmem_limit_bytes=32 * 1024 * 1024),
        cost_estimate=pl.CostEstimate(flops=1_100_000_000, bytes_accessed=4_000_000, transcendentals=0),
        name="gram_tile",
    )(place, *left, *right)


def add_up(*terms):
    total = terms[0].astype(jnp.float32)
    for term in terms[1:]:
        total = total + term.astype(jnp.float32)
    return total


def narrow(*terms):
    return add_up(*terms).astype(jnp.bfloat16)


def per_device(features, coef, labels, sign_bits, samples):
    my_zh, my_x, my_c = lax.axis_index("zh"), lax.axis_index("x"), lax.axis_index("c")
    my_zl, my_y = lax.axis_index("zl"), lax.axis_index("y")
    root_total = jnp.sqrt(jnp.float32(ROWS * 32))

    other_features = ring("c", features, 1)
    integers = jnp.concatenate([samples, sign_bits[None], labels[None]], axis=0)
    other_integers = ring("c", integers, 1)

    partial_value = jnp.dot(features, coef, preferred_element_type=jnp.float32).reshape(32, 128)
    everyone = lax.all_to_all(jnp.broadcast_to(partial_value, (16, 32, 128)), ("c", "zl", "y"), 0, 0).reshape(2, 8, 32, 128)
    by_core = [sum(everyone[core, k] for k in range(8)) for core in range(2)]
    margins = jnp.where(my_c == 0, by_core[0], by_core[1])
    other_margins = jnp.where(my_c == 0, by_core[1], by_core[0])

    def row_terms(value, bits, targets):
        probability = jax.nn.sigmoid(value)
        scale = jnp.sqrt(probability * (1.0 - probability))
        factor = (2.0 * bits.reshape(32, 128).astype(jnp.float32) - 1.0) * scale
        return factor.reshape(HIGH, LOW), (probability - targets.reshape(32, 128).astype(jnp.float32)).reshape(HIGH, LOW)

    terms = [row_terms(margins, sign_bits, labels), row_terms(other_margins, other_integers[1], other_integers[2])]
    factors, residuals = (jnp.concatenate(pair, axis=0) for pair in zip(*terms))

    picks = jnp.stack([integers[0], other_integers[0]]).reshape(2, 4, 4, 2, 2, 64)
    picks = lax.dynamic_index_in_dim(picks, my_c, axis=3, keepdims=False)
    picks = jnp.roll(picks, (-my_zh, -my_x), axis=(1, 2))
    picks = picks.transpose(0, 2, 3, 1, 4).reshape(4096)
    spots = (picks >> 3) * 64 + (picks & 7)

    *pieces, gradient = sketch_pieces(spots, features, other_features, factors, residuals)
    gradient = gradient[:, 0, :].reshape(8, 128)
    piece = [[pieces[2 * b + h].reshape(4, HALF_PAIRS, 16, 128) for h in range(2)] for b in range(4)]

    def swap_add(axis_name, flip, value):
        return value + lax.ppermute(value, axis_name, [(i, i ^ flip) for i in range(4)])

    far_0, far_1 = ring("x", piece[2][0], 1), ring("x", piece[2][1], -1)
    after_1, before_0 = ring("x", piece[1][1], 1), ring("x", piece[3][0], -1)
    gradient = swap_add("zh", 1, gradient)
    far_0, far_1, gradient = lax.optimization_barrier((far_0, far_1, gradient))
    after_0 = ring("x", narrow(piece[1][0], far_0), 1)
    before_1 = ring("x", narrow(piece[3][1], far_1), -1)
    gradient = swap_add("zh", 2, gradient)
    after_1, before_0, gradient = lax.optimization_barrier((after_1, before_0, gradient))
    wide = [
        [add_up(piece[0][0][a], after_0[a], before_0[a]), add_up(piece[0][1][a], after_1[a], before_1[a])]
        for a in range(4)
    ]
    short = [[half.astype(jnp.bfloat16) for half in pair] for pair in wide]
    from_last = ring("zh", jnp.stack([short[2][0], short[1][1]]), 1)
    from_next = ring("zh", jnp.stack([short[2][1], short[3][0]]), -1)
    gradient = swap_add("x", 1, gradient)
    from_last, from_next, gradient = lax.optimization_barrier((from_last, from_next, gradient))
    end_0 = ring("zh", narrow(short[1][0], from_last[0]), 1)
    end_1 = ring("zh", narrow(short[3][1], from_next[0]), -1)
    gradient = swap_add("x", 2, gradient)
    end_0, end_1, gradient = lax.optimization_barrier((end_0, end_1, gradient))
    summed = [add_up(wide[0][0], from_next[1], end_0), add_up(wide[0][1], from_last[1], end_1)]
    summed = jnp.concatenate(summed, axis=0).reshape(128, COLS)
    sketch = (summed / root_total).astype(jnp.bfloat16)

    zh_last, zh_next = ring("zh", sketch, 1), ring("zh", sketch, -1)
    x_next, x_far, x_last = (ring("x", sketch, shift) for shift in (-1, 2, 1))
    zh_last, zh_next, x_last, x_next, x_far = lax.optimization_barrier((zh_last, zh_next, x_last, x_next, x_far))
    zh_far_0, zh_far_1 = ring("zh", zh_last[:64], 1), ring("zh", zh_next[64:], -1)
    left = [jnp.concatenate([sketch, x_next, x_far, x_last], axis=0)]
    own_rows = jnp.concatenate([sketch, zh_next, zh_far_0, zh_far_1, zh_last], axis=0)
    right = [own_rows, ring("c", own_rows, 1)]
    place = jnp.stack([my_zh, my_x, my_c]).astype(jnp.int32)
    tiles = gram_pieces(place, left, right)
    parts = lax.all_to_all(tiles, ("zl", "y"), 0, 0)
    over_feat = add_up(*(parts[k] for k in range(8))).astype(jnp.bfloat16)

    def deliver(i):
        moves = []
        for x in range(4):
            for y in range(4):
                to_x, to_y = ((x & 1) ^ i) * 2 + (y & 1), (y & 2) | (x >> 1)
                moves.append((x * 4 + y, to_x * 4 + to_y))
        return lax.ppermute(over_feat[i], ("x", "y"), moves).astype(jnp.float32)

    same, turned = deliver(0), deliver(1)
    upper = my_x >= 2
    gram = jnp.concatenate([jnp.where(upper, turned, same), jnp.where(upper, same, turned)], axis=1)
    gram = gram / jnp.float32(8 * COLS)
    gradient = gradient.reshape(COLS)
    return (gradient / root_total, sketch, gram)


def solution(mesh):
    fine = Mesh(mesh.devices.reshape(4, 4, 2, 2, 4), ("zh", "x", "c", "zl", "y"))
    row, feat = ("zh", "x", "c"), ("zl", "y")
    return jax.shard_map(
        per_device,
        mesh=fine,
        in_specs=(P(row, feat), P(feat), P(row), P(row), P(row, None)),
        out_specs=(P(feat), P(row, feat), P(row, feat)),
        check_vma=False,
    )
```

```python
import functools

import jax
import jax.numpy as jnp
from jax import lax
from jax.experimental import pallas as pl
from jax.experimental.pallas import tpu as pltpu
from jax.sharding import Mesh, PartitionSpec as P

ROWS = 4096
COLS = 1024
LOW = 256
HIGH = ROWS // LOW
GROUP = 256
LANE_TILES = COLS // 128
HALF_PAIRS = 32
UNROLL = 16
EXTRA = 16
MARGIN_ROWS = 1024


def ring(axis_name, value, shift):
    size = lax.axis_size(axis_name)
    return lax.ppermute(value, axis_name, [(i, (i + shift) % size) for i in range(size)])


def margin_kernel(rows_ref, coef_ref, out):
    step = pl.program_id(0)
    sums = lax.dot_general(
        coef_ref[...], rows_ref[...], (((1,), (1,)), ((), ())), preferred_element_type=jnp.float32
    )
    for part in range(MARGIN_ROWS // 128):
        out[:, pl.ds(step * (MARGIN_ROWS // 128) + part, 1), :] = sums[:, part * 128 : (part + 1) * 128].reshape(
            16, 1, 128
        )


def margin_parts(features, coef):
    return pl.pallas_call(
        margin_kernel,
        grid=(ROWS // MARGIN_ROWS,),
        in_specs=[
            pl.BlockSpec((MARGIN_ROWS, COLS), lambda i: (i, 0)),
            pl.BlockSpec((16, COLS), lambda i: (0, 0)),
        ],
        out_specs=pl.BlockSpec((16, ROWS // 128, 128), lambda i: (0, 0, 0)),
        out_shape=jax.ShapeDtypeStruct((16, ROWS // 128, 128), jnp.float32),
        compiler_params=pltpu.CompilerParams(vmem_limit_bytes=60 * 1024 * 1024),
        cost_estimate=pl.CostEstimate(flops=130_000_000, bytes_accessed=9_000_000, transcendentals=0),
        name="margin_parts",
    )(features, jnp.broadcast_to(coef, (16, COLS)))


def sketch_kernel(spots, own_ref, other_ref, factor_ref, residual_ref, *refs):
    outs, (gradient, table_rows, own_pass, other_pass, transformed) = refs[:8], refs[8:]
    step = pl.program_id(0)
    last = COLS // GROUP

    def multiply(block, high):
        source, target = ((own_ref, own_pass), (other_ref, other_pass))[block]
        product = jnp.dot(
            table_rows[block * HIGH + high],
            source[pl.ds(pl.multiple_of(high * LOW, LOW), LOW), :],
            preferred_element_type=jnp.float32,
        )
        target[high] = product[:LOW]
        gradient[step] += product[LOW : LOW + 8]

    def combine(block, group, tile_row):
        source = (own_pass, other_pass)[block]
        for lane_tile in range(GROUP // 128):
            rows = pl.ds(pl.multiple_of(tile_row * 8, 8), 8)
            values = [source[high, rows, lane_tile * 128 : (lane_tile + 1) * 128] for high in range(HIGH)]
            stride = 1
            while stride < HIGH:
                for high in range(HIGH):
                    if not high & stride:
                        a, b = values[high], values[high + stride]
                        values[high], values[high + stride] = a + b, a - b
                stride *= 2
            place = tile_row * 64 + (group * (GROUP // 128) + lane_tile) * 8
            for high in range(HIGH):
                transformed[block, pl.ds(pl.multiple_of(high * (LOW * 8) + place, 8), 8), :] = values[high]

    def run(multiplied, combined):
        def body(high, carry):
            if multiplied is not None:
                multiply(multiplied, high)
            if combined is not None:
                for tile in range(LOW // 8 // HIGH):
                    combine(*combined, high * (LOW // 8 // HIGH) + tile)
            return carry

        lax.fori_loop(0, HIGH, body, 0, unroll=UNROLL)

    @pl.when(step == 0)
    def _():
        both = lax.broadcasted_iota(jnp.int32, (LOW, LOW), 0) & lax.broadcasted_iota(jnp.int32, (LOW, LOW), 1)
        for bit in (4, 2, 1):
            both = both ^ (both >> bit)
        signs = (1 - 2 * (both & 1)).astype(jnp.float32)
        for part in range(2 * HIGH):
            table_rows[part, :LOW] = (signs * factor_ref[part : part + 1, :]).astype(jnp.bfloat16)
            table_rows[part, LOW:] = jnp.broadcast_to(residual_ref[part : part + 1, :], (EXTRA, LOW)).astype(
                jnp.bfloat16
            )
        gradient[...] = jnp.zeros_like(gradient)
        run(0, None)

    @pl.when((step > 0) & (step < last))
    def _():
        run(0, (1, step - 1))

    @pl.when(step < last)
    def _():
        run(1, (0, step))

    @pl.when(step == last)
    def _():
        run(None, (1, last - 1))
        start = 0
        for out in outs:
            pairs = out.shape[0]

            def pick(pair, carry, out=out, start=start):
                rows = []
                for member in range(2):
                    at = start + pair * 2 + member
                    rows.append(
                        transformed[0, pl.ds(spots[at], 8, 8), :]
                        + transformed[1, pl.ds(spots[2 * 1024 + at], 8, 8), :]
                    )
                out[pair] = jnp.concatenate(rows, axis=0).astype(jnp.bfloat16)
                return carry

            lax.fori_loop(0, pairs, pick, 0, unroll=16)
            start += 2 * pairs


def sketch_pieces(spots, own, other, factors, residuals):
    pairs = [4 * HALF_PAIRS] * 8
    last = COLS // GROUP - 1
    return pl.pallas_call(
        sketch_kernel,
        grid_spec=pltpu.PrefetchScalarGridSpec(
            num_scalar_prefetch=1,
            grid=(last + 2,),
            in_specs=[
                pl.BlockSpec((ROWS, GROUP), lambda i, s: (0, jnp.minimum(i, last))),
                pl.BlockSpec((ROWS, GROUP), lambda i, s: (0, jnp.minimum(i, last))),
                pl.BlockSpec((2 * HIGH, LOW), lambda i, s: (0, 0)),
                pl.BlockSpec((2 * HIGH, LOW), lambda i, s: (0, 0)),
            ],
            out_specs=[pl.BlockSpec((n, 16, 128), lambda i, s: (0, 0, 0)) for n in pairs]
            + [pl.BlockSpec((COLS // GROUP, 8, GROUP), lambda i, s: (0, 0, 0))],
            scratch_shapes=[
                pltpu.VMEM((2 * HIGH, LOW + EXTRA, LOW), jnp.bfloat16),
                pltpu.VMEM((HIGH, LOW, GROUP), jnp.float32),
                pltpu.VMEM((HIGH, LOW, GROUP), jnp.float32),
                pltpu.VMEM((2, ROWS * LANE_TILES + 64, 128), jnp.float32),
            ],
        ),
        out_shape=[jax.ShapeDtypeStruct((n, 16, 128), jnp.bfloat16) for n in pairs]
        + [jax.ShapeDtypeStruct((COLS // GROUP, 8, GROUP), jnp.float32)],
        compiler_params=pltpu.CompilerParams(vmem_limit_bytes=62 * 1024 * 1024),
        cost_estimate=pl.CostEstimate(flops=4_400_000_000, bytes_accessed=22_000_000, transcendentals=0),
        name="hadamard_pick",
    )(spots, own, other, factors, residuals)


def gram_kernel(place, left_ref, right_ref, *refs):
    earlier, out, tile = (refs[0], refs[1], refs[2]) if len(refs) == 3 else (None, *refs)
    my_zh, my_x, my_c = [place[i] for i in range(3)]
    product = lax.dot_general(
        left_ref[...], right_ref[...], (((1,), (1,)), ((), ())), preferred_element_type=jnp.float32
    ).astype(jnp.bfloat16)
    for shift in range(4):
        for row in range(4):
            tile[lax.rem(my_zh + shift, 4), lax.rem(my_x + row, 4)] = product[
                row * 128 : (row + 1) * 128, shift * 128 : (shift + 1) * 128
            ]
    for target in range(8):
        zh, x_low = target // 2, target % 2
        for i in range(2):
            block = tile[zh, lax.rem(my_x + i, 2) * 2 + x_low]
            if earlier is None:
                out[target, i] = block
            else:
                first = earlier[target, i]
                out[target, i, :, :128] = jnp.where(my_c == 0, first, block)
                out[target, i, :, 128:] = jnp.where(my_c == 0, block, first)


def gram_pieces(place, left, right, earlier=()):
    vmem = pl.BlockSpec(memory_space=pltpu.VMEM)
    return pl.pallas_call(
        gram_kernel,
        in_specs=[pl.BlockSpec(memory_space=pltpu.SMEM)] + [vmem] * (2 + len(earlier)),
        out_specs=vmem,
        out_shape=jax.ShapeDtypeStruct((8, 2, 128, 128 * (1 + len(earlier))), jnp.bfloat16),
        scratch_shapes=[pltpu.VMEM((4, 4, 128, 128), jnp.bfloat16)],
        compiler_params=pltpu.CompilerParams(vmem_limit_bytes=32 * 1024 * 1024),
        cost_estimate=pl.CostEstimate(flops=540_000_000, bytes_accessed=3_000_000, transcendentals=0),
        name="gram_tile",
    )(place, left, right, *earlier)


def add_up(*terms):
    total = terms[0].astype(jnp.float32)
    for term in terms[1:]:
        total = total + term.astype(jnp.float32)
    return total


def narrow(*terms):
    return add_up(*terms).astype(jnp.bfloat16)


def per_device(features, coef, labels, sign_bits, samples):
    my_zh, my_x, my_c = lax.axis_index("zh"), lax.axis_index("x"), lax.axis_index("c")
    my_zl, my_y = lax.axis_index("zl"), lax.axis_index("y")
    root_total = jnp.sqrt(jnp.float32(ROWS * 32))

    other_features = ring("c", features, 1)
    integers = jnp.concatenate([samples, sign_bits[None], labels[None]], axis=0)
    other_integers = ring("c", integers, 1)

    everyone = lax.all_to_all(margin_parts(features, coef), ("c", "zl", "y"), 0, 0).reshape(2, 8, 32, 128)
    by_core = [sum(everyone[core, k] for k in range(8)) for core in range(2)]
    margins = jnp.where(my_c == 0, by_core[0], by_core[1])
    other_margins = jnp.where(my_c == 0, by_core[1], by_core[0])

    def row_terms(value, bits, targets):
        probability = jax.nn.sigmoid(value)
        scale = jnp.sqrt(probability * (1.0 - probability))
        factor = (2.0 * bits.reshape(32, 128).astype(jnp.float32) - 1.0) * scale
        return factor.reshape(HIGH, LOW), (probability - targets.reshape(32, 128).astype(jnp.float32)).reshape(HIGH, LOW)

    terms = [row_terms(margins, sign_bits, labels), row_terms(other_margins, other_integers[1], other_integers[2])]
    factors, residuals = (jnp.concatenate(pair, axis=0) for pair in zip(*terms))

    picks = jnp.stack([integers[0], other_integers[0]]).reshape(2, 4, 4, 2, 2, 64)
    picks = lax.dynamic_index_in_dim(picks, my_c, axis=3, keepdims=False)
    picks = jnp.roll(picks, (-my_zh, -my_x), axis=(1, 2))
    picks = picks.transpose(0, 2, 3, 1, 4).reshape(4096)
    spots = (picks >> 3) * 64 + (picks & 7)

    *pieces, gradient = sketch_pieces(spots, features, other_features, factors, residuals)
    gradient = gradient[:, 0, :].reshape(8, 128)
    piece = [[pieces[2 * b + h].reshape(4, HALF_PAIRS, 16, 128) for h in range(2)] for b in range(4)]

    def swap_add(axis_name, flip, value):
        return value + lax.ppermute(value, axis_name, [(i, i ^ flip) for i in range(4)])

    far_0, far_1 = ring("x", piece[2][0], 1), ring("x", piece[2][1], -1)
    after_1, before_0 = ring("x", piece[1][1], 1), ring("x", piece[3][0], -1)
    gradient = swap_add("zh", 1, gradient)
    far_0, far_1, gradient = lax.optimization_barrier((far_0, far_1, gradient))
    after_0 = ring("x", narrow(piece[1][0], far_0), 1)
    before_1 = ring("x", narrow(piece[3][1], far_1), -1)
    gradient = swap_add("zh", 2, gradient)
    after_1, before_0, gradient = lax.optimization_barrier((after_1, before_0, gradient))
    wide = [
        [add_up(piece[0][0][a], after_0[a], before_0[a]), add_up(piece[0][1][a], after_1[a], before_1[a])]
        for a in range(4)
    ]
    short = [[half.astype(jnp.bfloat16) for half in pair] for pair in wide]
    from_last = ring("zh", jnp.stack([short[2][0], short[1][1]]), 1)
    from_next = ring("zh", jnp.stack([short[2][1], short[3][0]]), -1)
    gradient = swap_add("x", 1, gradient)
    from_last, from_next, gradient = lax.optimization_barrier((from_last, from_next, gradient))
    end_0 = ring("zh", narrow(short[1][0], from_last[0]), 1)
    end_1 = ring("zh", narrow(short[3][1], from_next[0]), -1)
    end_0, end_1 = lax.optimization_barrier((end_0, end_1))
    summed = [add_up(wide[0][0], from_next[1], end_0), add_up(wide[0][1], from_last[1], end_1)]
    summed = jnp.concatenate(summed, axis=0).reshape(128, COLS)
    sketch = (summed / root_total).astype(jnp.bfloat16)

    zh_last, zh_next = ring("zh", sketch, 1), ring("zh", sketch, -1)
    _, gradient = lax.optimization_barrier((sketch, gradient))
    gradient = swap_add("x", 2, gradient)
    for_x, gradient = lax.optimization_barrier((sketch, gradient))
    x_next, x_far, x_last = (ring("x", for_x, shift) for shift in (-1, 2, 1))
    zh_last, zh_next, x_last, x_next, x_far = lax.optimization_barrier((zh_last, zh_next, x_last, x_next, x_far))
    zh_far_0, zh_far_1 = ring("zh", zh_last[:64], 1), ring("zh", zh_next[64:], -1)
    left = jnp.concatenate([sketch, x_next, x_far, x_last], axis=0)
    own_rows = jnp.concatenate([sketch, zh_next, zh_far_0, zh_far_1, zh_last], axis=0)
    other_rows = ring("c", own_rows, 1)
    place = jnp.stack([my_zh, my_x, my_c]).astype(jnp.int32)
    own_tile = gram_pieces(place, left, own_rows)
    tiles = gram_pieces(place, left, other_rows, (own_tile,))
    parts = lax.all_to_all(tiles, ("zl", "y"), 0, 0)
    over_feat = add_up(*(parts[k] for k in range(8))).astype(jnp.bfloat16)

    def deliver(i):
        moves = []
        for x in range(4):
            for y in range(4):
                to_x, to_y = ((x & 1) ^ i) * 2 + (y & 1), (y & 2) | (x >> 1)
                moves.append((x * 4 + y, to_x * 4 + to_y))
        return lax.ppermute(over_feat[i], ("x", "y"), moves).astype(jnp.float32)

    same, turned = deliver(0), deliver(1)
    upper = my_x >= 2
    gram = jnp.concatenate([jnp.where(upper, turned, same), jnp.where(upper, same, turned)], axis=1)
    gram = gram / jnp.float32(8 * COLS)
    gradient = gradient.reshape(COLS)
    return (gradient / root_total, sketch, gram)


def solution(mesh):
    fine = Mesh(mesh.devices.reshape(4, 4, 2, 2, 4), ("zh", "x", "c", "zl", "y"))
    row, feat = ("zh", "x", "c"), ("zl", "y")
    return jax.shard_map(
        per_device,
        mesh=fine,
        in_specs=(P(row, feat), P(feat), P(row), P(row), P(row, None)),
        out_specs=(P(feat), P(row, feat), P(row, feat)),
        check_vma=False,
    )
```

```python
import functools

import jax
import jax.numpy as jnp
from jax import lax
from jax.experimental import pallas as pl
from jax.experimental.pallas import tpu as pltpu
from jax.sharding import Mesh, PartitionSpec as P

ROWS = 4096
COLS = 1024
LOW = 256
HIGH = ROWS // LOW
GROUP = 256
LANE_TILES = COLS // 128
HALF_PAIRS = 32
SPLIT = 1
EXTRA = 16


def ring(axis_name, value, shift):
    size = lax.axis_size(axis_name)
    return lax.ppermute(value, axis_name, [(i, (i + shift) % size) for i in range(size)])


def sketch_kernel(spots, *refs):
    own_refs, other_refs, (factor_ref, residual_ref) = refs[:SPLIT], refs[SPLIT : 2 * SPLIT], refs[2 * SPLIT : 2 * SPLIT + 2]
    refs = refs[2 * SPLIT + 2 :]
    outs, (gradient, table_rows, own_pass, other_pass, transformed) = refs[:8], refs[8:]
    step = pl.program_id(0)
    last = COLS // GROUP

    def multiply(block, high):
        sources, target = ((own_refs, own_pass), (other_refs, other_pass))[block]
        share = HIGH // SPLIT
        product = jnp.dot(
            table_rows[block * HIGH + high],
            sources[high // share][high % share * LOW : (high % share + 1) * LOW, :],
            preferred_element_type=jnp.float32,
        )
        target[high] = product[:LOW]
        return product[LOW : LOW + 8]

    def combine(block, group, tile_row):
        source = (own_pass, other_pass)[block]
        for lane_tile in range(GROUP // 128):
            rows = pl.ds(pl.multiple_of(tile_row * 8, 8), 8)
            values = [source[high, rows, lane_tile * 128 : (lane_tile + 1) * 128] for high in range(HIGH)]
            stride = 1
            while stride < HIGH:
                for high in range(HIGH):
                    if not high & stride:
                        a, b = values[high], values[high + stride]
                        values[high], values[high + stride] = a + b, a - b
                stride *= 2
            place = tile_row * 64 + (group * (GROUP // 128) + lane_tile) * 8
            for high in range(HIGH):
                transformed[block, pl.ds(pl.multiple_of(high * (LOW * 8) + place, 8), 8), :] = values[high]

    def run(multiplied, combined):
        extra = []
        for high in range(HIGH):
            if multiplied is not None:
                extra.append(multiply(multiplied, high))
            if combined is not None:
                for tile in range(LOW // 8 // HIGH):
                    combine(*combined, high * (LOW // 8 // HIGH) + tile)
        if extra:
            gradient[step] += sum(extra[1:], extra[0])

    @pl.when(step == 0)
    def _():
        both = lax.broadcasted_iota(jnp.int32, (LOW, LOW), 0) & lax.broadcasted_iota(jnp.int32, (LOW, LOW), 1)
        for bit in (4, 2, 1):
            both = both ^ (both >> bit)
        signs = (1 - 2 * (both & 1)).astype(jnp.float32)
        for part in range(2 * HIGH):
            table_rows[part, :LOW] = (signs * factor_ref[part : part + 1, :]).astype(jnp.bfloat16)
            table_rows[part, LOW:] = jnp.broadcast_to(residual_ref[part : part + 1, :], (EXTRA, LOW)).astype(
                jnp.bfloat16
            )
        gradient[...] = jnp.zeros_like(gradient)
        run(0, None)

    @pl.when((step > 0) & (step < last))
    def _():
        run(0, (1, step - 1))

    @pl.when(step < last)
    def _():
        run(1, (0, step))

    @pl.when(step == last)
    def _():
        run(None, (1, last - 1))
        start = 0
        for out in outs:
            pairs = out.shape[0]

            def pick(pair, carry, out=out, start=start):
                rows = []
                for member in range(2):
                    at = start + pair * 2 + member
                    rows.append(
                        transformed[0, pl.ds(spots[at], 8, 8), :]
                        + transformed[1, pl.ds(spots[2 * 1024 + at], 8, 8), :]
                    )
                out[pair] = jnp.concatenate(rows, axis=0).astype(jnp.bfloat16)
                return carry

            lax.fori_loop(0, pairs, pick, 0, unroll=32)
            start += 2 * pairs


def sketch_pieces(spots, own, other, factors, residuals):
    pairs = [4 * HALF_PAIRS] * 8
    last = COLS // GROUP - 1
    return pl.pallas_call(
        sketch_kernel,
        grid_spec=pltpu.PrefetchScalarGridSpec(
            num_scalar_prefetch=1,
            grid=(last + 2,),
            in_specs=[
                *[
                    pl.BlockSpec((ROWS // SPLIT, GROUP), lambda i, s, part=part: (part, jnp.minimum(i, last)))
                    for part in range(SPLIT)
                ]
                * 2,
                pl.BlockSpec((2 * HIGH, LOW), lambda i, s: (0, 0)),
                pl.BlockSpec((2 * HIGH, LOW), lambda i, s: (0, 0)),
            ],
            out_specs=[pl.BlockSpec((n, 16, 128), lambda i, s: (0, 0, 0)) for n in pairs]
            + [pl.BlockSpec((COLS // GROUP, 8, GROUP), lambda i, s: (0, 0, 0))],
            scratch_shapes=[
                pltpu.VMEM((2 * HIGH, LOW + EXTRA, LOW), jnp.bfloat16),
                pltpu.VMEM((HIGH, LOW, GROUP), jnp.float32),
                pltpu.VMEM((HIGH, LOW, GROUP), jnp.float32),
                pltpu.VMEM((2, ROWS * LANE_TILES + 64, 128), jnp.float32),
            ],
        ),
        out_shape=[jax.ShapeDtypeStruct((n, 16, 128), jnp.bfloat16) for n in pairs]
        + [jax.ShapeDtypeStruct((COLS // GROUP, 8, GROUP), jnp.float32)],
        compiler_params=pltpu.CompilerParams(vmem_limit_bytes=62 * 1024 * 1024),
        cost_estimate=pl.CostEstimate(flops=4_400_000_000, bytes_accessed=22_000_000, transcendentals=0),
        name="hadamard_pick",
    )(spots, *[own] * SPLIT, *[other] * SPLIT, factors, residuals)


def gram_kernel(place, left_ref, right_ref, *refs):
    earlier, out, tile = (refs[0], refs[1], refs[2]) if len(refs) == 3 else (None, *refs)
    my_zh, my_x, my_c = [place[i] for i in range(3)]
    product = lax.dot_general(
        left_ref[...], right_ref[...], (((1,), (1,)), ((), ())), preferred_element_type=jnp.float32
    ).astype(jnp.bfloat16)
    for shift in range(4):
        for row in range(4):
            tile[lax.rem(my_zh + shift, 4), lax.rem(my_x + row, 4)] = product[
                row * 128 : (row + 1) * 128, shift * 128 : (shift + 1) * 128
            ]
    for target in range(8):
        zh, x_low = target // 2, target % 2
        for i in range(2):
            block = tile[zh, lax.rem(my_x + i, 2) * 2 + x_low]
            if earlier is None:
                out[target, i] = block
            else:
                first = earlier[target, i]
                out[target, i, :, :128] = jnp.where(my_c == 0, first, block)
                out[target, i, :, 128:] = jnp.where(my_c == 0, block, first)


def gram_pieces(place, left, right, earlier=()):
    vmem = pl.BlockSpec(memory_space=pltpu.VMEM)
    return pl.pallas_call(
        gram_kernel,
        in_specs=[pl.BlockSpec(memory_space=pltpu.SMEM)] + [vmem] * (2 + len(earlier)),
        out_specs=vmem,
        out_shape=jax.ShapeDtypeStruct((8, 2, 128, 128 * (1 + len(earlier))), jnp.bfloat16),
        scratch_shapes=[pltpu.VMEM((4, 4, 128, 128), jnp.bfloat16)],
        compiler_params=pltpu.CompilerParams(vmem_limit_bytes=32 * 1024 * 1024),
        cost_estimate=pl.CostEstimate(flops=540_000_000, bytes_accessed=3_000_000, transcendentals=0),
        name="gram_tile",
    )(place, left, right, *earlier)


def add_up(*terms):
    total = terms[0].astype(jnp.float32)
    for term in terms[1:]:
        total = total + term.astype(jnp.float32)
    return total


def narrow(*terms):
    return add_up(*terms).astype(jnp.bfloat16)


def per_device(features, coef, labels, sign_bits, samples):
    my_zh, my_x, my_c = lax.axis_index("zh"), lax.axis_index("x"), lax.axis_index("c")
    my_zl, my_y = lax.axis_index("zl"), lax.axis_index("y")
    root_total = jnp.sqrt(jnp.float32(ROWS * 32))

    other_features = ring("c", features, 1)
    integers = jnp.concatenate([samples, sign_bits[None], labels[None]], axis=0)
    other_integers = ring("c", integers, 1)

    partial_value = jnp.dot(features, coef, preferred_element_type=jnp.float32).reshape(32, 128)
    partial_sum = partial_value
    for shift in (1, 2, 3):
        partial_sum = partial_sum + ring("y", partial_value, shift)
    pairs = [(c * 2 + l, c, l) for c in range(2) for l in range(2)]

    def swap(flip_c, flip_l):
        return lax.ppermute(partial_sum, ("c", "zl"), [(i, (c ^ flip_c) * 2 + (l ^ flip_l)) for i, c, l in pairs])

    margins = partial_sum + swap(0, 1)
    other_margins = swap(1, 0) + swap(1, 1)

    def row_terms(value, bits, targets):
        probability = jax.nn.sigmoid(value)
        scale = jnp.sqrt(probability * (1.0 - probability))
        factor = (2.0 * bits.reshape(32, 128).astype(jnp.float32) - 1.0) * scale
        return factor.reshape(HIGH, LOW), (probability - targets.reshape(32, 128).astype(jnp.float32)).reshape(HIGH, LOW)

    terms = [row_terms(margins, sign_bits, labels), row_terms(other_margins, other_integers[1], other_integers[2])]
    factors, residuals = (jnp.concatenate(pair, axis=0) for pair in zip(*terms))

    picks = jnp.stack([integers[0], other_integers[0]]).reshape(2, 4, 4, 2, 2, 64)
    picks = lax.dynamic_index_in_dim(picks, my_c, axis=3, keepdims=False)
    picks = jnp.roll(picks, (-my_zh, -my_x), axis=(1, 2))
    picks = picks.transpose(0, 2, 3, 1, 4).reshape(4096)
    spots = (picks >> 3) * 64 + (picks & 7)

    *pieces, gradient = sketch_pieces(spots, features, other_features, factors, residuals)
    gradient = gradient[:, 0, :].reshape(8, 128)
    piece = [[pieces[2 * b + h].reshape(4, HALF_PAIRS, 16, 128) for h in range(2)] for b in range(4)]

    def swap_add(axis_name, flip, value):
        return value + lax.ppermute(value, axis_name, [(i, i ^ flip) for i in range(4)])

    far_0, far_1 = ring("x", piece[2][0], 1), ring("x", piece[2][1], -1)
    after_1, before_0 = ring("x", piece[1][1], 1), ring("x", piece[3][0], -1)
    gradient = swap_add("zh", 1, gradient)
    far_0, far_1, gradient = lax.optimization_barrier((far_0, far_1, gradient))
    after_0 = ring("x", narrow(piece[1][0], far_0), 1)
    before_1 = ring("x", narrow(piece[3][1], far_1), -1)
    gradient = swap_add("zh", 2, gradient)
    after_1, before_0, gradient = lax.optimization_barrier((after_1, before_0, gradient))
    wide = [
        [add_up(piece[0][0][a], after_0[a], before_0[a]), add_up(piece[0][1][a], after_1[a], before_1[a])]
        for a in range(4)
    ]
    short = [[half.astype(jnp.bfloat16) for half in pair] for pair in wide]
    end_far_0, end_far_1 = ring("zh", short[2][0], 1), ring("zh", short[2][1], -1)
    end_after_1, end_before_0 = ring("zh", short[1][1], 1), ring("zh", short[3][0], -1)
    end_far_0, end_far_1 = lax.optimization_barrier((end_far_0, end_far_1))
    end_after_0 = ring("zh", narrow(short[1][0], end_far_0), 1)
    end_before_1 = ring("zh", narrow(short[3][1], end_far_1), -1)
    gradient = swap_add("x", 1, gradient)
    end_after_1, end_before_0, gradient = lax.optimization_barrier((end_after_1, end_before_0, gradient))
    end_after_0, end_before_1 = lax.optimization_barrier((end_after_0, end_before_1))
    summed = [add_up(wide[0][0], end_before_0, end_after_0), add_up(wide[0][1], end_after_1, end_before_1)]
    summed = jnp.concatenate(summed, axis=0).reshape(128, COLS)
    sketch = (summed / root_total).astype(jnp.bfloat16)

    zh_last, zh_next = ring("zh", sketch, 1), ring("zh", sketch, -1)
    _, gradient = lax.optimization_barrier((sketch, gradient))
    gradient = swap_add("x", 2, gradient)
    for_x, gradient = lax.optimization_barrier((sketch, gradient))
    x_last, x_next = ring("x", for_x, 1), ring("x", for_x, -1)
    zh_last, zh_next, x_last, x_next = lax.optimization_barrier((zh_last, zh_next, x_last, x_next))
    zh_far_0, zh_far_1 = ring("zh", zh_last[:64], 1), ring("zh", zh_next[64:], -1)
    x_far_0, x_far_1 = ring("x", x_last[:64], 1), ring("x", x_next[64:], -1)
    zh_far_0, zh_far_1, x_far_0, x_far_1 = lax.optimization_barrier((zh_far_0, zh_far_1, x_far_0, x_far_1))
    left = jnp.concatenate([sketch, x_next, x_far_0, x_far_1, x_last], axis=0)
    own_rows = jnp.concatenate([sketch, zh_next, zh_far_0, zh_far_1, zh_last], axis=0)
    other_rows = ring("c", own_rows, 1)
    place = jnp.stack([my_zh, my_x, my_c]).astype(jnp.int32)
    own_tile = gram_pieces(place, left, own_rows)
    tiles = gram_pieces(place, left, other_rows, (own_tile,))
    parts = lax.all_to_all(tiles, ("zl", "y"), 0, 0)
    over_feat = add_up(*(parts[k] for k in range(8))).astype(jnp.bfloat16)

    def deliver(i):
        moves = []
        for x in range(4):
            for y in range(4):
                to_x, to_y = ((x & 1) ^ i) * 2 + (y & 1), (y & 2) | (x >> 1)
                moves.append((x * 4 + y, to_x * 4 + to_y))
        return lax.ppermute(over_feat[i], ("x", "y"), moves).astype(jnp.float32)

    same, turned = deliver(0), deliver(1)
    upper = my_x >= 2
    gram = jnp.concatenate([jnp.where(upper, turned, same), jnp.where(upper, same, turned)], axis=1)
    gram = gram / jnp.float32(8 * COLS)
    gradient = gradient.reshape(COLS)
    return (gradient / root_total, sketch, gram)


def solution(mesh):
    fine = Mesh(mesh.devices.reshape(4, 4, 2, 2, 4), ("zh", "x", "c", "zl", "y"))
    row, feat = ("zh", "x", "c"), ("zl", "y")
    return jax.shard_map(
        per_device,
        mesh=fine,
        in_specs=(P(row, feat), P(feat), P(row), P(row), P(row, None)),
        out_specs=(P(feat), P(row, feat), P(row, feat)),
        check_vma=False,
    )
```

```python
import functools

import jax
import jax.numpy as jnp
from jax import lax
from jax.experimental import pallas as pl
from jax.experimental.pallas import tpu as pltpu
from jax.sharding import Mesh, PartitionSpec as P

ROWS = 4096
COLS = 1024
LOW = 256
HIGH = ROWS // LOW
GROUP = 256
LANE_TILES = COLS // 128
HALF_PAIRS = 32
SPLIT = 1
EXTRA = 16


def ring(axis_name, value, shift):
    size = lax.axis_size(axis_name)
    return lax.ppermute(value, axis_name, [(i, (i + shift) % size) for i in range(size)])


def sketch_kernel(spots, *refs):
    own_refs, other_refs, (factor_ref, residual_ref) = refs[:SPLIT], refs[SPLIT : 2 * SPLIT], refs[2 * SPLIT : 2 * SPLIT + 2]
    refs = refs[2 * SPLIT + 2 :]
    outs, (gradient, table_rows, own_pass, other_pass, transformed) = refs[:8], refs[8:]
    step = pl.program_id(0)
    last = COLS // GROUP

    def multiply(block, high):
        sources, target = ((own_refs, own_pass), (other_refs, other_pass))[block]
        share = HIGH // SPLIT
        product = jnp.dot(
            table_rows[block * HIGH + high],
            sources[high // share][high % share * LOW : (high % share + 1) * LOW, :],
            preferred_element_type=jnp.float32,
        )
        target[high] = product[:LOW]
        return product[LOW : LOW + 8]

    def combine(block, group, tile_row):
        source = (own_pass, other_pass)[block]
        for lane_tile in range(GROUP // 128):
            rows = pl.ds(pl.multiple_of(tile_row * 8, 8), 8)
            values = [source[high, rows, lane_tile * 128 : (lane_tile + 1) * 128] for high in range(HIGH)]
            stride = 1
            while stride < HIGH:
                for high in range(HIGH):
                    if not high & stride:
                        a, b = values[high], values[high + stride]
                        values[high], values[high + stride] = a + b, a - b
                stride *= 2
            place = tile_row * 64 + (group * (GROUP // 128) + lane_tile) * 8
            for high in range(HIGH):
                transformed[block, pl.ds(pl.multiple_of(high * (LOW * 8) + place, 8), 8), :] = values[high]

    def run(multiplied, combined):
        extra = []
        for high in range(HIGH):
            if multiplied is not None:
                extra.append(multiply(multiplied, high))
            if combined is not None:
                for tile in range(LOW // 8 // HIGH):
                    combine(*combined, high * (LOW // 8 // HIGH) + tile)
        if extra:
            gradient[step] += sum(extra[1:], extra[0])

    @pl.when(step == 0)
    def _():
        both = lax.broadcasted_iota(jnp.int32, (LOW, LOW), 0) & lax.broadcasted_iota(jnp.int32, (LOW, LOW), 1)
        for bit in (4, 2, 1):
            both = both ^ (both >> bit)
        signs = (1 - 2 * (both & 1)).astype(jnp.float32)
        for part in range(2 * HIGH):
            table_rows[part, :LOW] = (signs * factor_ref[part : part + 1, :]).astype(jnp.bfloat16)
            table_rows[part, LOW:] = jnp.broadcast_to(residual_ref[part : part + 1, :], (EXTRA, LOW)).astype(
                jnp.bfloat16
            )
        gradient[...] = jnp.zeros_like(gradient)
        run(0, None)

    @pl.when((step > 0) & (step < last))
    def _():
        run(0, (1, step - 1))

    @pl.when(step < last)
    def _():
        run(1, (0, step))

    @pl.when(step == last)
    def _():
        run(None, (1, last - 1))
        start = 0
        for out in outs:
            pairs = out.shape[0]

            def pick(pair, carry, out=out, start=start):
                rows = []
                for member in range(2):
                    at = start + pair * 2 + member
                    rows.append(
                        transformed[0, pl.ds(spots[at], 8, 8), :]
                        + transformed[1, pl.ds(spots[2 * 1024 + at], 8, 8), :]
                    )
                out[pair] = jnp.concatenate(rows, axis=0).astype(jnp.bfloat16)
                return carry

            lax.fori_loop(0, pairs, pick, 0, unroll=32)
            start += 2 * pairs


def sketch_pieces(spots, own, other, factors, residuals):
    pairs = [4 * HALF_PAIRS] * 8
    last = COLS // GROUP - 1
    return pl.pallas_call(
        sketch_kernel,
        grid_spec=pltpu.PrefetchScalarGridSpec(
            num_scalar_prefetch=1,
            grid=(last + 2,),
            in_specs=[
                *[
                    pl.BlockSpec((ROWS // SPLIT, GROUP), lambda i, s, part=part: (part, jnp.minimum(i, last)))
                    for part in range(SPLIT)
                ]
                * 2,
                pl.BlockSpec((2 * HIGH, LOW), lambda i, s: (0, 0)),
                pl.BlockSpec((2 * HIGH, LOW), lambda i, s: (0, 0)),
            ],
            out_specs=[pl.BlockSpec((n, 16, 128), lambda i, s: (0, 0, 0)) for n in pairs]
            + [pl.BlockSpec((COLS // GROUP, 8, GROUP), lambda i, s: (0, 0, 0))],
            scratch_shapes=[
                pltpu.VMEM((2 * HIGH, LOW + EXTRA, LOW), jnp.bfloat16),
                pltpu.VMEM((HIGH, LOW, GROUP), jnp.float32),
                pltpu.VMEM((HIGH, LOW, GROUP), jnp.float32),
                pltpu.VMEM((2, ROWS * LANE_TILES + 64, 128), jnp.float32),
            ],
        ),
        out_shape=[jax.ShapeDtypeStruct((n, 16, 128), jnp.bfloat16) for n in pairs]
        + [jax.ShapeDtypeStruct((COLS // GROUP, 8, GROUP), jnp.float32)],
        compiler_params=pltpu.CompilerParams(vmem_limit_bytes=62 * 1024 * 1024),
        cost_estimate=pl.CostEstimate(flops=4_400_000_000, bytes_accessed=22_000_000, transcendentals=0),
        name="hadamard_pick",
    )(spots, *[own] * SPLIT, *[other] * SPLIT, factors, residuals)


def gram_kernel(place, left_ref, right_ref, *refs):
    earlier, out, tile = (refs[0], refs[1], refs[2]) if len(refs) == 3 else (None, *refs)
    my_zh, my_x, my_c = [place[i] for i in range(3)]
    product = lax.dot_general(
        left_ref[...], right_ref[...], (((1,), (1,)), ((), ())), preferred_element_type=jnp.float32
    ).astype(jnp.bfloat16)
    for shift in range(4):
        for row in range(4):
            tile[lax.rem(my_zh + shift, 4), lax.rem(my_x + row, 4)] = product[
                row * 128 : (row + 1) * 128, shift * 128 : (shift + 1) * 128
            ]
    for target in range(8):
        zh, x_low = target // 2, target % 2
        for i in range(2):
            block = tile[zh, lax.rem(my_x + i, 2) * 2 + x_low]
            if earlier is None:
                out[target, i] = block
            else:
                first = earlier[target, i]
                out[target, i, :, :128] = jnp.where(my_c == 0, first, block)
                out[target, i, :, 128:] = jnp.where(my_c == 0, block, first)


def gram_pieces(place, left, right, earlier=()):
    vmem = pl.BlockSpec(memory_space=pltpu.VMEM)
    return pl.pallas_call(
        gram_kernel,
        in_specs=[pl.BlockSpec(memory_space=pltpu.SMEM)] + [vmem] * (2 + len(earlier)),
        out_specs=vmem,
        out_shape=jax.ShapeDtypeStruct((8, 2, 128, 128 * (1 + len(earlier))), jnp.bfloat16),
        scratch_shapes=[pltpu.VMEM((4, 4, 128, 128), jnp.bfloat16)],
        compiler_params=pltpu.CompilerParams(vmem_limit_bytes=32 * 1024 * 1024),
        cost_estimate=pl.CostEstimate(flops=540_000_000, bytes_accessed=3_000_000, transcendentals=0),
        name="gram_tile",
    )(place, left, right, *earlier)


def add_up(*terms):
    total = terms[0].astype(jnp.float32)
    for term in terms[1:]:
        total = total + term.astype(jnp.float32)
    return total


def narrow(*terms):
    return add_up(*terms).astype(jnp.bfloat16)


def per_device(features, coef, labels, sign_bits, samples):
    my_zh, my_x, my_c = lax.axis_index("zh"), lax.axis_index("x"), lax.axis_index("c")
    my_zl, my_y = lax.axis_index("zl"), lax.axis_index("y")
    root_total = jnp.sqrt(jnp.float32(ROWS * 32))

    other_features = ring("c", features, 1)
    integers = jnp.concatenate([samples, sign_bits[None], labels[None]], axis=0)
    other_integers = ring("c", integers, 1)

    partial_value = jnp.dot(features, coef, preferred_element_type=jnp.float32).reshape(32, 128)
    partial_sum = partial_value
    for shift in (1, 2, 3):
        partial_sum = partial_sum + ring("y", partial_value, shift)
    pairs = [(c * 2 + l, c, l) for c in range(2) for l in range(2)]

    def swap(flip_c, flip_l):
        return lax.ppermute(partial_sum, ("c", "zl"), [(i, (c ^ flip_c) * 2 + (l ^ flip_l)) for i, c, l in pairs])

    margins = partial_sum + swap(0, 1)
    other_margins = swap(1, 0) + swap(1, 1)

    def row_terms(value, bits, targets):
        probability = jax.nn.sigmoid(value)
        scale = jnp.sqrt(probability * (1.0 - probability))
        factor = (2.0 * bits.reshape(32, 128).astype(jnp.float32) - 1.0) * scale
        return factor.reshape(HIGH, LOW), (probability - targets.reshape(32, 128).astype(jnp.float32)).reshape(HIGH, LOW)

    terms = [row_terms(margins, sign_bits, labels), row_terms(other_margins, other_integers[1], other_integers[2])]
    factors, residuals = (jnp.concatenate(pair, axis=0) for pair in zip(*terms))

    picks = jnp.stack([integers[0], other_integers[0]]).reshape(2, 4, 4, 2, 2, 64)
    picks = lax.dynamic_index_in_dim(picks, my_c, axis=3, keepdims=False)
    picks = jnp.roll(picks, (-my_zh, -my_x), axis=(1, 2))
    picks = picks.transpose(0, 2, 3, 1, 4).reshape(4096)
    spots = (picks >> 3) * 64 + (picks & 7)

    *pieces, gradient = sketch_pieces(spots, features, other_features, factors, residuals)
    piece = [[pieces[2 * b + h].reshape(4, HALF_PAIRS, 16, 128) for h in range(2)] for b in range(4)]

    def swap_add(axis_name, flip, value):
        return value + lax.ppermute(value, axis_name, [(i, i ^ flip) for i in range(4)])

    far_0, far_1 = ring("x", piece[2][0], 1), ring("x", piece[2][1], -1)
    after_1, before_0 = ring("x", piece[1][1], 1), ring("x", piece[3][0], -1)
    gradient = swap_add("zh", 1, gradient)
    far_0, far_1, gradient = lax.optimization_barrier((far_0, far_1, gradient))
    after_0 = ring("x", narrow(piece[1][0], far_0), 1)
    before_1 = ring("x", narrow(piece[3][1], far_1), -1)
    gradient = swap_add("zh", 2, gradient)
    gradient = swap_add("x", 1, gradient)
    after_1, before_0, gradient = lax.optimization_barrier((after_1, before_0, gradient))
    wide = [
        [add_up(piece[0][0][a], after_0[a], before_0[a]), add_up(piece[0][1][a], after_1[a], before_1[a])]
        for a in range(4)
    ]
    short = [[half.astype(jnp.bfloat16) for half in pair] for pair in wide]
    end_far_0, end_far_1 = ring("zh", short[2][0], 1), ring("zh", short[2][1], -1)
    end_after_1, end_before_0 = ring("zh", short[1][1], 1), ring("zh", short[3][0], -1)
    end_far_0, end_far_1 = lax.optimization_barrier((end_far_0, end_far_1))
    end_after_0 = ring("zh", narrow(short[1][0], end_far_0), 1)
    end_before_1 = ring("zh", narrow(short[3][1], end_far_1), -1)
    end_after_0, end_before_1 = lax.optimization_barrier((end_after_0, end_before_1))
    summed = [add_up(wide[0][0], end_before_0, end_after_0), add_up(wide[0][1], end_after_1, end_before_1)]
    summed = jnp.concatenate(summed, axis=0).reshape(128, COLS)
    sketch = (summed / root_total).astype(jnp.bfloat16)

    zh_last, zh_next = ring("zh", sketch, 1), ring("zh", sketch, -1)
    _, gradient = lax.optimization_barrier((sketch, gradient))
    gradient = swap_add("x", 2, gradient)
    for_x, gradient = lax.optimization_barrier((sketch, gradient))
    x_last, x_next = ring("x", for_x, 1), ring("x", for_x, -1)
    zh_last, zh_next, x_last, x_next = lax.optimization_barrier((zh_last, zh_next, x_last, x_next))
    zh_far_0, zh_far_1 = ring("zh", zh_last[:64], 1), ring("zh", zh_next[64:], -1)
    x_far_0, x_far_1 = ring("x", x_last[:64], 1), ring("x", x_next[64:], -1)
    zh_far_0, zh_far_1, x_far_0, x_far_1 = lax.optimization_barrier((zh_far_0, zh_far_1, x_far_0, x_far_1))
    left = jnp.concatenate([sketch, x_next, x_far_0, x_far_1, x_last], axis=0)
    own_rows = jnp.concatenate([sketch, zh_next, zh_far_0, zh_far_1, zh_last], axis=0)
    other_rows = ring("c", own_rows, 1)
    place = jnp.stack([my_zh, my_x, my_c]).astype(jnp.int32)
    own_tile = gram_pieces(place, left, own_rows)
    tiles = gram_pieces(place, left, other_rows, (own_tile,))
    parts = lax.all_to_all(tiles, ("zl", "y"), 0, 0)
    over_feat = add_up(*(parts[k] for k in range(8))).astype(jnp.bfloat16)

    def deliver(i):
        moves = []
        for x in range(4):
            for y in range(4):
                to_x, to_y = ((x & 1) ^ i) * 2 + (y & 1), (y & 2) | (x >> 1)
                moves.append((x * 4 + y, to_x * 4 + to_y))
        return lax.ppermute(over_feat[i], ("x", "y"), moves).astype(jnp.float32)

    same, turned = deliver(0), deliver(1)
    upper = my_x >= 2
    gram = jnp.concatenate([jnp.where(upper, turned, same), jnp.where(upper, same, turned)], axis=1)
    gram = gram / jnp.float32(8 * COLS)
    gradient = gradient[:, 0, :].reshape(COLS)
    return (gradient / root_total, sketch, gram)


def solution(mesh):
    fine = Mesh(mesh.devices.reshape(4, 4, 2, 2, 4), ("zh", "x", "c", "zl", "y"))
    row, feat = ("zh", "x", "c"), ("zl", "y")
    return jax.shard_map(
        per_device,
        mesh=fine,
        in_specs=(P(row, feat), P(feat), P(row), P(row), P(row, None)),
        out_specs=(P(feat), P(row, feat), P(row, feat)),
        check_vma=False,
    )
```
